32 devices in a mesh: grp: 2 (over x), blk: 16 (over z, y, core).
Axes of the slice: x: 2, y: 2, z: 4, core: 2. Of those that a mesh axis runs over, the one named last changes fastest.
Arguments:
- example_grads: bfloat16 [256, 131072], P('grp', 'blk'), parts along dimension 0, may hold values from -6 to 6
- tile_seeds: int32 [256, 8], P('blk'), may hold values from 0 to 16777215
- pair_index: int32 [128, 2], P('grp'), parts along dimension 0, may hold values from 0 to 127
Outputs:
- projected: float32 [4096, 256], P('blk', 'grp'), parts along dimension 1
- scores: float32 [128], P('grp'), parts along dimension 0
The draws below stay inside these ranges and needn't reach their ends.
There are 2 independent parts, one for each index of `grp`. The reference program is written for one: setup_inputs(seed, part) draws one part's arguments, and reference() takes and returns one part's arrays. A program takes and returns all parts, laid end to end along the dimension named above; an argument that names none is the same for every part. Nothing has to cross between parts.
Inputs may be any that keep to these rules, and one draw needn't show every extreme that they name: `pair_index`: column 0 names the query example and column 1 the negative example.
All inputs are finite; a program needn't handle non-finite values.
Results may differ from the reference program's by a relative error of at most 0.0003.
Values sent between devices are 32-bit elements; how exact they have to be, the bound alone decides.
A program may use at most 64 MiB of HBM per device.

```python
import math
import jax
import jax.numpy as jnp
from jax import lax

K = 4096
TILE = 512
PAIRS = 64
EX = 128
P_SIZE = 131072


def touch_ends(entries, own_key, least, top_value):
    longest = entries.shape.index(max(entries.shape))
    spots = []
    for shift in (0, 1):
        where = [jax.random.randint(jax.random.fold_in(own_key, axis), (), 0, length) for axis, length in enumerate(entries.shape)]
        where[longest] = (where[longest] + shift) % entries.shape[longest]
        spots.append(tuple(where))
    return entries.at[spots[0]].set(least).at[spots[1]].set(top_value)


def steps_of(key, shape, pieces, least, largest):
    def one(position, blocks):
        heights = jax.random.uniform(jax.random.fold_in(jax.random.fold_in(key, 6), position), (blocks,), jnp.float32, least / len(pieces), largest / len(pieces))
        return jnp.repeat(jnp.exp(heights), shape[position] // blocks).reshape((-1,) + (1,) * (len(shape) - position - 1))

    factor_of = one(*pieces[0])
    for cut in pieces[1:]:
        factor_of = factor_of * one(*cut)
    return factor_of


def normal_values(rng, extent, spread, limit, pieces=(), kind=jnp.bfloat16):
    level = steps_of(rng, extent, pieces, -0.22, 0.18) if pieces else 1.0
    drawn = jax.random.normal(rng, extent, jnp.float32) * spread * level
    return jnp.minimum(jnp.maximum(drawn, -limit), limit).astype(kind)


def setup_inputs(seed: int = 0, part: int = 0) -> dict:
    keys = jax.random.split(jax.random.key(seed), 4)
    own_keys = jax.random.split(jax.random.fold_in(keys[3], part), 4)
    return {
        "example_grads": normal_values(own_keys[0], (EX, P_SIZE), 1.0, 6.0, ((1, 16),)),
        "tile_seeds": touch_ends(jax.random.randint(keys[1], (P_SIZE // TILE, K // TILE), 0, 16777216), jax.random.fold_in(keys[1], 1), 0, 16777215).astype(jnp.int32),
        "pair_index": touch_ends(jax.random.randint(own_keys[2], (PAIRS, 2), 0, EX), jax.random.fold_in(own_keys[2], 1), 0, EX - 1).astype(jnp.int32),
    }


golden_mult = -1640531535
mixer_one = -2048144789
mixer_two = -1028477387

def hashed(seed_value, flat_index):
    mixed = seed_value ^ flat_index * jnp.int32(golden_mult)
    mixed = mixed ^ lax.shift_right_logical(mixed, jnp.int32(16))
    mixed = mixed * jnp.int32(mixer_one)
    mixed = mixed ^ lax.shift_right_logical(mixed, jnp.int32(13))
    mixed = mixed * jnp.int32(mixer_two)
    mixed = mixed ^ lax.shift_right_logical(mixed, jnp.int32(16))
    bit_value = lax.shift_right_logical(mixed, jnp.int32(15)) & jnp.int32(1)
    return jnp.int32(1) - jnp.int32(2) * bit_value

def reference(example_grads, tile_seeds, pair_index):
    examples, params = example_grads.shape
    tile_count = params // TILE
    col_within = jnp.arange(K, dtype=jnp.int32) % TILE
    row_ids = jnp.arange(TILE, dtype=jnp.int32)
    flat_index = row_ids[:, None] * TILE + col_within[None, :]

    def advance(running, tile_pos):
        seed_row = lax.dynamic_index_in_dim(tile_seeds, tile_pos, 0, keepdims=False)
        seed_cols = jnp.broadcast_to(seed_row[:, None], (K // TILE, TILE)).reshape(K)
        sign_tile = hashed(seed_cols[None, :], flat_index).astype(jnp.bfloat16)
        grad_block = lax.dynamic_slice_in_dim(example_grads, tile_pos * TILE, TILE, 1)
        running = running + lax.dot_general(sign_tile, grad_block, (((0,), (1,)), ((), ())), preferred_element_type=jnp.float32)
        return (running, None)
    running, unused = lax.scan(advance, jnp.zeros((K, examples), jnp.float32), jnp.arange(tile_count, dtype=jnp.int32))
    projected = running * (1.0 / math.sqrt(params))
    query_cols = projected[:, pair_index[:, 0]]
    negative_cols = projected[:, pair_index[:, 1]]
    scores = lax.optimization_barrier(jnp.sum(query_cols * negative_cols, axis=0)) * (1.0 / math.sqrt(K))
    return (projected, scores)
```

```python
import functools
import math

import jax
import jax.numpy as jnp
from jax import lax
from jax.experimental import pallas as pl
from jax.experimental.pallas import tpu as pltpu
from jax.sharding import PartitionSpec as P

TILE = 512
ROWS = 256

golden_mult = -1640531535
mixer_one = -2048144789
mixer_two = -1028477387


def fill_table(table):
    def rows(start, carry):
        base = pl.multiple_of(start * 8, 8)
        col = lax.broadcasted_iota(jnp.int32, (8, TILE), 0) + base
        row = lax.broadcasted_iota(jnp.int32, (8, TILE), 1)
        mixed = (row * TILE + col) * jnp.int32(golden_mult)
        table[pl.ds(base, 8), :] = mixed ^ lax.shift_right_logical(mixed, jnp.int32(16))
        return carry

    lax.fori_loop(0, TILE // 8, rows, 0)


def signs(entries, seed):
    mixed = (entries ^ seed) * jnp.int32(mixer_one)
    mixed = mixed ^ lax.shift_right_logical(mixed, jnp.int32(13))
    mixed = mixed * jnp.int32(mixer_two)
    mixed = mixed ^ lax.shift_right_logical(mixed, jnp.int32(16))
    low = mixed.astype(jnp.int16)
    return jnp.where(low < 0, jnp.bfloat16(-1), jnp.bfloat16(1))


def kernel(
    devices, scaling,
    seeds, grads, pairs, own_ref, score_ref,
    table, part, sib, summed, arrive, score_send, score_recv,
    sib_s, sib_r, out_s, out_r, sc_s, sc_r,
):
    me = lax.axis_index("blk")
    core = lax.rem(me, 2)
    chip = lax.div(me, 2)
    chips = devices // 2
    sibling = me + 1 - 2 * core
    own, examples = own_ref.shape
    width = 2 * own
    step_rows = min(width, ROWS)
    row_tiles = seeds.shape[0]

    barrier = pltpu.get_barrier_semaphore()

    def greet(shift, carry):
        pl.semaphore_signal(
            barrier, inc=1, device_id={"blk": lax.rem(me + shift, devices)},
            device_id_type=pl.DeviceIdType.MESH,
        )
        return carry

    lax.fori_loop(1, devices, greet, 0)
    fill_table(table)

    def target(step):
        return lax.rem(chip + 1 + step, chips)

    def compute(step):
        start = target(step) * width
        tile_col = lax.div(start, TILE)
        within = lax.rem(start, TILE)

        def row_tile(pos, carry):
            seed = seeds[pos, tile_col]
            seed = seed ^ lax.shift_right_logical(seed, jnp.int32(16))
            block = grads[:, pl.ds(pl.multiple_of(pos * TILE, TILE), TILE)]
            for piece in range(width // step_rows):
                at = pl.multiple_of(within + piece * step_rows, step_rows)
                sign = signs(table[pl.ds(at, step_rows), :], seed)
                add = lax.dot_general(
                    sign, block, (((1,), (1,)), ((), ())),
                    preferred_element_type=jnp.float32,
                )
                rows = pl.ds(piece * step_rows, step_rows)
                part[step, rows, :] += add
            return carry

        part[step] = jnp.zeros((width, examples), jnp.float32)
        lax.fori_loop(0, row_tiles, row_tile, 0)

    def half(which):
        return pl.ds(pl.multiple_of(which * own, own), own)

    def sib_copy(step):
        return pltpu.make_async_remote_copy(
            src_ref=part.at[step, half(1 - core), :],
            dst_ref=sib.at[step],
            send_sem=sib_s.at[step],
            recv_sem=sib_r.at[step],
            device_id={"blk": sibling},
            device_id_type=pl.DeviceIdType.MESH,
        )

    def out_copy(step):
        return pltpu.make_async_remote_copy(
            src_ref=summed.at[step],
            dst_ref=arrive.at[step],
            send_sem=out_s.at[step],
            recv_sem=out_r.at[step],
            device_id={"blk": target(step) * 2 + core},
            device_id_type=pl.DeviceIdType.MESH,
        )

    def forward(step):
        sib_copy(step).wait()
        summed[step] = part[step, half(core), :] + sib[step]
        out_copy(step).start()

    compute(0)
    pl.semaphore_wait(barrier, devices - 1)
    sib_copy(0).start()

    def advance(step, carry):
        compute(step)
        sib_copy(step).start()
        forward(step - 1)
        return carry

    lax.fori_loop(1, chips, advance, 0)
    last = chips - 1
    sib_copy(last).wait()
    own_ref[...] = part[last, half(core), :] + sib[last]

    def gather(step, carry):
        out_copy(step).wait()
        own_ref[...] += arrive[step]
        return carry

    lax.fori_loop(0, last, gather, 0)

    ids = lax.broadcasted_iota(jnp.int32, (pairs.shape[0], examples), 1)
    columns = own_ref[...] * scaling

    def pick(which):
        chosen = jnp.where(pairs[:, which : which + 1] == ids, 1.0, 0.0)
        return lax.dot_general(
            columns, chosen, (((1,), (1,)), ((), ())),
            precision=lax.Precision.HIGHEST,
            preferred_element_type=jnp.float32,
        )

    share = jnp.sum(pick(0) * pick(1), axis=0, keepdims=True)
    score_send[...] = jnp.zeros_like(score_send)
    score_send[0:1, 0 : pairs.shape[0]] = share

    def score_copy(shift):
        return pltpu.make_async_remote_copy(
            src_ref=score_send,
            dst_ref=score_recv.at[shift],
            send_sem=sc_s.at[shift],
            recv_sem=sc_r.at[shift],
            device_id={"blk": lax.rem(me + shift, devices)},
            device_id_type=pl.DeviceIdType.MESH,
        )

    def score_start(shift, carry):
        score_copy(shift).start()
        return carry

    lax.fori_loop(1, devices, score_start, 0)
    score_ref[...] = score_send[...]

    def score_finish(shift, carry):
        score_copy(shift).wait()
        score_ref[...] += score_recv[shift]
        return carry

    lax.fori_loop(1, devices, score_finish, 0)


def per_device(example_grads, tile_seeds, pair_index):
    examples, params = example_grads.shape
    devices = lax.axis_size("blk")
    col_total = tile_seeds.shape[1] * TILE
    scaling = 1.0 / math.sqrt(params * devices)
    own = col_total // devices
    chips = devices // 2
    pairs = pair_index.shape[0]
    lanes = -(-pairs // 128) * 128
    vmem = pl.BlockSpec(memory_space=pltpu.VMEM)
    own_rows, shares = pl.pallas_call(
        functools.partial(kernel, devices, scaling),
        out_shape=(
            jax.ShapeDtypeStruct((own, examples), jnp.float32),
            jax.ShapeDtypeStruct((8, lanes), jnp.float32),
        ),
        in_specs=[pl.BlockSpec(memory_space=pltpu.SMEM), vmem, vmem],
        out_specs=(vmem, vmem),
        scratch_shapes=[
            pltpu.VMEM((TILE, TILE), jnp.int32),
            pltpu.VMEM((chips, 2 * own, examples), jnp.float32),
            pltpu.VMEM((chips, own, examples), jnp.float32),
            pltpu.VMEM((chips, own, examples), jnp.float32),
            pltpu.VMEM((chips, own, examples), jnp.float32),
            pltpu.VMEM((8, lanes), jnp.float32),
            pltpu.VMEM((devices, 8, lanes), jnp.float32),
            pltpu.SemaphoreType.DMA((chips,)),
            pltpu.SemaphoreType.DMA((chips,)),
            pltpu.SemaphoreType.DMA((chips,)),
            pltpu.SemaphoreType.DMA((chips,)),
            pltpu.SemaphoreType.DMA((devices,)),
            pltpu.SemaphoreType.DMA((devices,)),
        ],
        compiler_params=pltpu.CompilerParams(
            collective_id=0, has_side_effects=True, vmem_limit_bytes=40 * 1024 * 1024
        ),
        cost_estimate=pl.CostEstimate(
            flops=2 * col_total * params * examples,
            bytes_accessed=2 * params * examples,
            transcendentals=0,
        ),
    )(tile_seeds, example_grads, pair_index)
    scores = shares[0, :pairs] * (1.0 / math.sqrt(col_total))
    return (own_rows * scaling, scores)


def solution(mesh):
    placed = (P("grp", "blk"), P("blk", None), P("grp", None))
    return jax.shard_map(
        per_device,
        mesh=mesh,
        in_specs=placed,
        out_specs=(P("blk", "grp"), P("grp")),
        check_vma=False,
    )
```

```python
import functools
import math

import jax
import jax.numpy as jnp
from jax import lax
from jax.experimental import pallas as pl
from jax.experimental.pallas import tpu as pltpu
from jax.sharding import PartitionSpec as P

TILE = 512
ROWS = 16

golden_mult = -1640531535
mixer_one = -2048144789
mixer_two = -1028477387


def fill_table(table):
    def rows(start, carry):
        base = pl.multiple_of(start * 8, 8)
        col = lax.broadcasted_iota(jnp.int32, (8, TILE), 0) + base
        row = lax.broadcasted_iota(jnp.int32, (8, TILE), 1)
        mixed = (row * TILE + col) * jnp.int32(golden_mult)
        table[pl.ds(base, 8), :] = mixed ^ lax.shift_right_logical(mixed, jnp.int32(16))
        return carry

    lax.fori_loop(0, TILE // 8, rows, 0)


def signs(entries, seed):
    mixed = (entries ^ seed) * jnp.int32(mixer_one)
    mixed = mixed ^ lax.shift_right_logical(mixed, jnp.int32(13))
    mixed = mixed * jnp.int32(mixer_two)
    mixed = mixed ^ lax.shift_right_logical(mixed, jnp.int32(16))
    low = mixed.astype(jnp.int16)
    return jnp.where(low < 0, jnp.bfloat16(-1), jnp.bfloat16(1))


def kernel(
    devices, scaling,
    seeds_in, grads_in, pairs_in, own_ref, score_ref,
    seeds, grads, pairs, in_sem, table, even, odd, part, sib, summed, arrive, score_send, score_recv,
    sib_s, sib_r, out_s, out_r, sc_s, sc_r,
):
    me = lax.axis_index("blk")
    core = lax.rem(me, 2)
    chip = lax.div(me, 2)
    chips = devices // 2
    sibling = me + 1 - 2 * core
    own, examples = own_ref.shape
    width = 2 * own
    row_tiles = seeds.shape[1]

    loads = [
        pltpu.make_async_copy(source, held, in_sem.at[place])
        for place, (source, held) in enumerate(
            ((seeds_in, seeds), (grads_in, grads), (pairs_in, pairs))
        )
    ]
    for load in loads:
        load.start()

    barrier = pltpu.get_barrier_semaphore()

    def greet(shift, carry):
        pl.semaphore_signal(
            barrier, inc=1, device_id={"blk": lax.rem(me + shift, devices)},
            device_id_type=pl.DeviceIdType.MESH,
        )
        return carry

    lax.fori_loop(1, devices, greet, 0)
    fill_table(table)

    def target(step):
        return lax.rem(chip + 1 + step, chips)

    def hash_tile(step, pos, signs_ref):
        start = target(step + lax.div(pos, row_tiles)) * width
        seed = seeds[lax.div(start, TILE), lax.rem(pos, row_tiles)]
        seed = seed ^ lax.shift_right_logical(seed, jnp.int32(16))
        within = 0 if width == TILE else lax.rem(start, TILE)
        for piece in range(width // ROWS):
            at = within + piece * ROWS
            if width != TILE:
                at = pl.multiple_of(at, ROWS)
            signs_ref[piece * ROWS : (piece + 1) * ROWS, :] = signs(
                table[pl.ds(at, ROWS), :], seed
            )

    def multiply(step, pos, signs_ref):
        block = grads[:, pl.ds(pl.multiple_of(pos * TILE, TILE), TILE)]
        part[step] += lax.dot_general(
            signs_ref[...], block, (((1,), (1,)), ((), ())),
            preferred_element_type=jnp.float32,
        )

    def compute(step):
        part[step] = jnp.zeros((width, examples), jnp.float32)

        def two_tiles(index, carry):
            pos = index * 2
            hash_tile(step, pos + 1, odd)
            multiply(step, pos, even)
            hash_tile(step, pos + 2, even)
            multiply(step, pos + 1, odd)
            return carry

        lax.fori_loop(0, row_tiles // 2, two_tiles, 0)

    def half(which):
        return pl.ds(pl.multiple_of(which * own, own), own)

    def sib_copy(step):
        return pltpu.make_async_remote_copy(
            src_ref=part.at[step, half(1 - core), :],
            dst_ref=sib.at[step],
            send_sem=sib_s.at[step],
            recv_sem=sib_r.at[step],
            device_id={"blk": sibling},
            device_id_type=pl.DeviceIdType.MESH,
        )

    def out_copy(step):
        return pltpu.make_async_remote_copy(
            src_ref=summed.at[step],
            dst_ref=arrive.at[step],
            send_sem=out_s.at[step],
            recv_sem=out_r.at[step],
            device_id={"blk": target(step) * 2 + core},
            device_id_type=pl.DeviceIdType.MESH,
        )

    def forward(step):
        sib_copy(step).wait()
        summed[step] = part[step, half(core), :] + sib[step]
        out_copy(step).start()

    loads[0].wait()
    hash_tile(0, 0, even)
    loads[1].wait()
    loads[2].wait()
    compute(0)
    pl.semaphore_wait(barrier, devices - 1)
    sib_copy(0).start()

    def advance(step, carry):
        compute(step)
        sib_copy(step).start()
        forward(step - 1)
        return carry

    lax.fori_loop(1, chips, advance, 0)
    last = chips - 1
    sib_copy(last).wait()
    own_ref[...] = part[last, half(core), :] + sib[last]

    def gather(step, carry):
        out_copy(step).wait()
        own_ref[...] += arrive[step]
        return carry

    lax.fori_loop(0, last, gather, 0)

    count = pairs.shape[1]
    ids = lax.broadcasted_iota(jnp.int32, (examples, count), 0)
    columns = own_ref[...] * scaling

    def pick(which):
        chosen = jnp.where(pairs[which : which + 1, :] == ids, 1.0, 0.0)
        return lax.dot_general(
            columns, chosen, (((1,), (0,)), ((), ())),
            precision=lax.Precision.HIGHEST,
            preferred_element_type=jnp.float32,
        )

    share = jnp.sum(pick(0) * pick(1), axis=0, keepdims=True)
    score_send[...] = jnp.zeros_like(score_send)
    score_send[0:1, 0:count] = share

    def score_copy(shift):
        return pltpu.make_async_remote_copy(
            src_ref=score_send,
            dst_ref=score_recv.at[shift],
            send_sem=sc_s.at[shift],
            recv_sem=sc_r.at[shift],
            device_id={"blk": lax.rem(me + shift, devices)},
            device_id_type=pl.DeviceIdType.MESH,
        )

    def score_start(shift, carry):
        score_copy(shift).start()
        return carry

    lax.fori_loop(1, devices, score_start, 0)
    score_ref[...] = score_send[...]

    def score_finish(shift, carry):
        score_copy(shift).wait()
        score_ref[...] += score_recv[shift]
        return carry

    lax.fori_loop(1, devices, score_finish, 0)


def per_device(example_grads, tile_seeds, pair_index):
    examples, params = example_grads.shape
    devices = lax.axis_size("blk")
    col_total = tile_seeds.shape[1] * TILE
    scaling = 1.0 / math.sqrt(params * devices)
    own = col_total // devices
    chips = devices // 2
    pairs = pair_index.shape[0]
    lanes = -(-pairs // 128) * 128
    vmem = pl.BlockSpec(memory_space=pltpu.VMEM)
    own_rows, shares = pl.pallas_call(
        functools.partial(kernel, devices, scaling),
        out_shape=(
            jax.ShapeDtypeStruct((own, examples), jnp.float32),
            jax.ShapeDtypeStruct((8, lanes), jnp.float32),
        ),
        in_specs=[pl.BlockSpec(memory_space=pl.ANY)] * 3,
        out_specs=(vmem, vmem),
        scratch_shapes=[
            pltpu.SMEM(tile_seeds.shape[::-1], jnp.int32),
            pltpu.VMEM((examples, params), example_grads.dtype),
            pltpu.VMEM(pair_index.shape[::-1], jnp.int32),
            pltpu.SemaphoreType.DMA((3,)),
            pltpu.VMEM((TILE, TILE), jnp.int32),
            pltpu.VMEM((2 * own, TILE), jnp.bfloat16),
            pltpu.VMEM((2 * own, TILE), jnp.bfloat16),
            pltpu.VMEM((chips, 2 * own, examples), jnp.float32),
            pltpu.VMEM((chips, own, examples), jnp.float32),
            pltpu.VMEM((chips, own, examples), jnp.float32),
            pltpu.VMEM((chips, own, examples), jnp.float32),
            pltpu.VMEM((8, lanes), jnp.float32),
            pltpu.VMEM((devices, 8, lanes), jnp.float32),
            pltpu.SemaphoreType.DMA((chips,)),
            pltpu.SemaphoreType.DMA((chips,)),
            pltpu.SemaphoreType.DMA((chips,)),
            pltpu.SemaphoreType.DMA((chips,)),
            pltpu.SemaphoreType.DMA((devices,)),
            pltpu.SemaphoreType.DMA((devices,)),
        ],
        compiler_params=pltpu.CompilerParams(
            collective_id=0, has_side_effects=True, vmem_limit_bytes=60 * 1024 * 1024
        ),
        cost_estimate=pl.CostEstimate(
            flops=2 * col_total * params * examples,
            bytes_accessed=2 * params * examples,
            transcendentals=0,
        ),
    )(tile_seeds.T, example_grads, pair_index.T)
    scores = shares[0, :pairs] * (1.0 / math.sqrt(col_total))
    return (own_rows * scaling, scores)


def solution(mesh):
    placed = (P("grp", "blk"), P("blk", None), P("grp", None))
    return jax.shard_map(
        per_device,
        mesh=mesh,
        in_specs=placed,
        out_specs=(P("blk", "grp"), P("grp")),
        check_vma=False,
    )
```

```python
import functools
import math

import jax
import jax.numpy as jnp
from jax import lax
from jax.experimental import pallas as pl
from jax.experimental.pallas import tpu as pltpu
from jax.sharding import PartitionSpec as P

TILE = 512
ROWS = 16

golden_mult = -1640531535
mixer_one = -2048144789
mixer_two = -1028477387


def fill_table(table):
    def rows(start, carry):
        base = pl.multiple_of(start * 8, 8)
        col = lax.broadcasted_iota(jnp.int32, (8, TILE), 0) + base
        row = lax.broadcasted_iota(jnp.int32, (8, TILE), 1)
        mixed = (row * TILE + col) * jnp.int32(golden_mult)
        table[pl.ds(base, 8), :] = mixed ^ lax.shift_right_logical(mixed, jnp.int32(16))
        return carry

    lax.fori_loop(0, TILE // 8, rows, 0)


def signs(entries, seed):
    mixed = (entries ^ seed) * jnp.int32(mixer_one)
    mixed = mixed ^ lax.shift_right_logical(mixed, jnp.int32(13))
    mixed = mixed * jnp.int32(mixer_two)
    mixed = mixed ^ lax.shift_right_logical(mixed, jnp.int32(16))
    low = mixed.astype(jnp.int16)
    return jnp.where(low < 0, jnp.bfloat16(-1), jnp.bfloat16(1))


def kernel(
    devices, scaling,
    seeds_in, grads_in, pairs_in, own_ref, score_ref,
    seeds, grads, pairs, in_sem, table, even, odd, part, sib, summed, arrive, score_send, score_recv,
    sib_s, sib_r, out_s, out_r, sc_s, sc_r,
):
    me = lax.axis_index("blk")
    core = lax.rem(me, 2)
    chip = lax.div(me, 2)
    chips = devices // 2
    sibling = me + 1 - 2 * core
    own, examples = own_ref.shape
    width = 2 * own
    row_tiles = seeds.shape[1]

    loads = [
        pltpu.make_async_copy(source, held, in_sem.at[place])
        for place, (source, held) in enumerate(
            ((seeds_in, seeds), (grads_in, grads), (pairs_in, pairs))
        )
    ]
    for load in loads:
        load.start()

    barrier = pltpu.get_barrier_semaphore()

    def greet(shift, carry):
        pl.semaphore_signal(
            barrier, inc=1, device_id={"blk": lax.rem(me + shift, devices)},
            device_id_type=pl.DeviceIdType.MESH,
        )
        return carry

    lax.fori_loop(1, devices, greet, 0)
    fill_table(table)

    def target(step):
        return lax.rem(chip + 1 + step, chips)

    def hash_tile(step, pos, signs_ref, first=0, parts=1):
        start = target(step + lax.div(pos, row_tiles)) * width
        seed = seeds[lax.div(start, TILE), lax.rem(pos, row_tiles)]
        seed = seed ^ lax.shift_right_logical(seed, jnp.int32(16))
        within = 0 if width == TILE else lax.rem(start, TILE)
        pieces = width // ROWS
        for piece in range(pieces * first // parts, pieces * (first + 1) // parts):
            at = within + piece * ROWS
            if width != TILE:
                at = pl.multiple_of(at, ROWS)
            signs_ref[piece * ROWS : (piece + 1) * ROWS, :] = signs(
                table[pl.ds(at, ROWS), :], seed
            )

    def multiply_and_hash(step, pos, ready, filled):
        depth = TILE // 2
        for part_pos in range(2):
            at = pl.multiple_of(pos * TILE + part_pos * depth, depth)
            part[step] += lax.dot_general(
                ready[:, part_pos * depth : (part_pos + 1) * depth],
                grads[:, pl.ds(at, depth)],
                (((1,), (1,)), ((), ())),
                preferred_element_type=jnp.float32,
            )
            hash_tile(step, pos + 1, filled, part_pos, 2)

    def compute(step, between):
        part[step] = jnp.zeros((width, examples), jnp.float32)

        def two_tiles(index, carry):
            multiply_and_hash(step, index * 2, even, odd)
            multiply_and_hash(step, index * 2 + 1, odd, even)
            return carry

        rounds = row_tiles // 2
        lax.fori_loop(0, rounds // 4, two_tiles, 0)
        between()
        lax.fori_loop(rounds // 4, rounds, two_tiles, 0)

    def half(which):
        return pl.ds(pl.multiple_of(which * own, own), own)

    def sib_copy(step):
        return pltpu.make_async_remote_copy(
            src_ref=part.at[step, half(1 - core), :],
            dst_ref=sib.at[step],
            send_sem=sib_s.at[step],
            recv_sem=sib_r.at[step],
            device_id={"blk": sibling},
            device_id_type=pl.DeviceIdType.MESH,
        )

    def out_copy(step):
        return pltpu.make_async_remote_copy(
            src_ref=summed.at[step],
            dst_ref=arrive.at[step],
            send_sem=out_s.at[step],
            recv_sem=out_r.at[step],
            device_id={"blk": target(step) * 2 + core},
            device_id_type=pl.DeviceIdType.MESH,
        )

    def forward(step):
        sib_copy(step).wait()
        summed[step] = part[step, half(core), :] + sib[step]
        out_copy(step).start()

    loads[0].wait()
    hash_tile(0, 0, even)
    loads[1].wait()
    loads[2].wait()
    compute(0, lambda: None)
    pl.semaphore_wait(barrier, devices - 1)
    sib_copy(0).start()

    def advance(step, carry):
        compute(step, lambda: forward(step - 1))
        sib_copy(step).start()
        return carry

    lax.fori_loop(1, chips, advance, 0)
    last = chips - 1
    sib_copy(last).wait()
    own_ref[...] = part[last, half(core), :] + sib[last]

    def gather(step, carry):
        out_copy(step).wait()
        own_ref[...] += arrive[step]
        return carry

    lax.fori_loop(0, last, gather, 0)

    count = pairs.shape[1]
    ids = lax.broadcasted_iota(jnp.int32, (examples, count), 0)
    columns = own_ref[...] * scaling

    def pick(which):
        chosen = jnp.where(pairs[which : which + 1, :] == ids, 1.0, 0.0)
        return lax.dot_general(
            columns, chosen, (((1,), (0,)), ((), ())),
            precision=lax.Precision.HIGHEST,
            preferred_element_type=jnp.float32,
        )

    share = jnp.sum(pick(0) * pick(1), axis=0, keepdims=True)
    score_send[...] = jnp.zeros_like(score_send)
    score_send[0:1, 0:count] = share

    def score_copy(shift):
        return pltpu.make_async_remote_copy(
            src_ref=score_send,
            dst_ref=score_recv.at[shift],
            send_sem=sc_s.at[shift],
            recv_sem=sc_r.at[shift],
            device_id={"blk": lax.rem(me + shift, devices)},
            device_id_type=pl.DeviceIdType.MESH,
        )

    def score_start(shift, carry):
        score_copy(shift).start()
        return carry

    lax.fori_loop(1, devices, score_start, 0)
    score_ref[...] = score_send[...]

    def score_finish(shift, carry):
        score_copy(shift).wait()
        score_ref[...] += score_recv[shift]
        return carry

    lax.fori_loop(1, devices, score_finish, 0)


def per_device(example_grads, tile_seeds, pair_index):
    examples, params = example_grads.shape
    devices = lax.axis_size("blk")
    col_total = tile_seeds.shape[1] * TILE
    scaling = 1.0 / math.sqrt(params * devices)
    own = col_total // devices
    chips = devices // 2
    pairs = pair_index.shape[0]
    lanes = -(-pairs // 128) * 128
    vmem = pl.BlockSpec(memory_space=pltpu.VMEM)
    own_rows, shares = pl.pallas_call(
        functools.partial(kernel, devices, scaling),
        out_shape=(
            jax.ShapeDtypeStruct((own, examples), jnp.float32),
            jax.ShapeDtypeStruct((8, lanes), jnp.float32),
        ),
        in_specs=[pl.BlockSpec(memory_space=pl.ANY)] * 3,
        out_specs=(vmem, vmem),
        scratch_shapes=[
            pltpu.SMEM(tile_seeds.shape[::-1], jnp.int32),
            pltpu.VMEM((examples, params), example_grads.dtype),
            pltpu.VMEM(pair_index.shape[::-1], jnp.int32),
            pltpu.SemaphoreType.DMA((3,)),
            pltpu.VMEM((TILE, TILE), jnp.int32),
            pltpu.VMEM((2 * own, TILE), jnp.bfloat16),
            pltpu.VMEM((2 * own, TILE), jnp.bfloat16),
            pltpu.VMEM((chips, 2 * own, examples), jnp.float32),
            pltpu.VMEM((chips, own, examples), jnp.float32),
            pltpu.VMEM((chips, own, examples), jnp.float32),
            pltpu.VMEM((chips, own, examples), jnp.float32),
            pltpu.VMEM((8, lanes), jnp.float32),
            pltpu.VMEM((devices, 8, lanes), jnp.float32),
            pltpu.SemaphoreType.DMA((chips,)),
            pltpu.SemaphoreType.DMA((chips,)),
            pltpu.SemaphoreType.DMA((chips,)),
            pltpu.SemaphoreType.DMA((chips,)),
            pltpu.SemaphoreType.DMA((devices,)),
            pltpu.SemaphoreType.DMA((devices,)),
        ],
        compiler_params=pltpu.CompilerParams(
            collective_id=0, has_side_effects=True, vmem_limit_bytes=60 * 1024 * 1024
        ),
        cost_estimate=pl.CostEstimate(
            flops=2 * col_total * params * examples,
            bytes_accessed=2 * params * examples,
            transcendentals=0,
        ),
    )(tile_seeds.T, example_grads, pair_index.T)
    scores = shares[0, :pairs] * (1.0 / math.sqrt(col_total))
    return (own_rows * scaling, scores)


def solution(mesh):
    placed = (P("grp", "blk"), P("blk", None), P("grp", None))
    return jax.shard_map(
        per_device,
        mesh=mesh,
        in_specs=placed,
        out_specs=(P("blk", "grp"), P("grp")),
        check_vma=False,
    )
```
